256 devices in a mesh: dcn: 2 (over x_hi), gx: 16 (over x_lo, y, core), gy: 8 (over z).
Axes of the slice: x: 4 (x_hi: 2, x_lo: 2; x = x_hi * 2 + x_lo), y: 4, z: 8, core: 2. Of those that a mesh axis runs over, the one named last changes fastest.
Arguments:
- hidden_in: bfloat16 [262144, 5376], P(('dcn', 'gx', 'gy')), may hold values from -24 to 24
- key_cotangent: bfloat16 [262144, 1024], P(('dcn', 'gx', 'gy')), may hold values from -6 to 6
Outputs:
- key_grad: float32 [5376, 1024], P(('gx', 'gy'))
The draws below stay inside these ranges and needn't reach their ends.
All inputs are finite; a program needn't handle non-finite values.
Results may differ from the reference program's by a relative error of at most 0.0003.
Values sent between devices are 32-bit elements; how exact they have to be, the bound alone decides.
No kernel may reach another device: no remote copies, remote signals or barrier semaphores. Data moves between devices by JAX's collectives and lax.ppermute only.
A program may use at most 128 MiB of HBM per device.

```python
import jax
import jax.numpy as jnp

D = 5376
KEYS = 1024
TOKENS = 262144


def spiked(values, key, source, target, parts, factor):
    owner, partner = [(jnp.arange(values.shape[dim]) // (values.shape[dim] // parts)).reshape([-1 if axis == dim else 1 for axis in range(values.ndim)]) for dim in (source, target)]
    chosen = jax.random.permutation(key, parts)[partner]
    strong = (owner == chosen) | (owner == (partner + parts // 2) % parts)
    return jnp.where(strong, factor * values, values)


def block_scale(own_key, dims, cuts, least, largest):
    def one(dim, parts):
        steps = jax.random.uniform(jax.random.fold_in(jax.random.fold_in(own_key, 6), dim), (parts,), jnp.float32, least / len(cuts), largest / len(cuts))
        return jnp.repeat(jnp.exp(steps), dims[dim] // parts).reshape((-1,) + (1,) * (len(dims) - dim - 1))

    level = one(*cuts[0])
    for cut in cuts[1:]:
        level = level * one(*cut)
    return level


def bell_draw(own_key, dims, scale, limit, pieces=(), held_as=jnp.bfloat16):
    result = jax.random.normal(own_key, dims, jnp.float32) * scale
    if len(pieces) > 0:
        result = block_scale(own_key, dims, pieces, -0.22, 0.18) * result
    return jnp.clip(result, min=-limit, max=limit).astype(held_as)


def gaussian_with(own_key, dims, deviation, reach, shards, heavy, dtype=jnp.bfloat16):
    entries = deviation * jax.random.normal(own_key, dims, jnp.float32)
    if shards:
        entries = entries * block_scale(own_key, dims, shards, -0.22, 0.18)
    return jnp.clip(spiked(entries, jax.random.fold_in(own_key, 3), *heavy), -reach, reach).astype(dtype)


def setup_inputs(seed: int = 0) -> dict:
    key_list = jax.random.split(jax.random.key(seed), 3)
    return {
        "hidden_in": gaussian_with(key_list[0], (TOKENS, D), 1.0, 24.0, ((0, 256),), (0, 1, 256, 6.0)),
        "key_cotangent": bell_draw(key_list[1], (TOKENS, KEYS), 1.0, 6.0, ((0, 256),)),
    }


def reference(hidden_in, key_cotangent):
    raw_grad = jnp.dot(hidden_in.T, key_cotangent, preferred_element_type=jnp.float32)
    return raw_grad * jnp.float32(1.0 / (TOKENS ** 0.5))
```

```python
import jax
import jax.numpy as jnp
from jax import lax
from jax.experimental import pallas as pl
from jax.experimental.pallas import tpu as pltpu
from jax.sharding import PartitionSpec as P

AXES = ("dcn", "gx", "gy")
ROWS = 7
STEP = 256

OFF_X = (320, 80, 0, 112)
OFF_Y = (352, 144, 32, 176)
OFF_Z = (304, 272, 240, 208, 64, 224, 256, 288)
CUT1, CUT2, UNITS = 80, 240, 384


def pick(table, k):
    value = jnp.int32(table[0])
    for i in range(1, len(table)):
        value = jnp.where(k == i, jnp.int32(table[i]), value)
    return value


def coords():
    dcn, gx, gy = (lax.axis_index(a) for a in AXES)
    core = lax.rem(gx, 2)
    y = lax.rem(lax.div(gx, 2), 4)
    x = dcn * 2 + lax.div(gx, 8)
    return x, y, gy, core


def grad_kernel(where_ref, h_ref, c_ref, keep, send1, send2, send3, acc, sem):
    i = pl.program_id(0)
    x, y, z, core = where_ref[0], where_ref[1], where_ref[2], where_ref[3]
    prod = lax.dot_general(
        h_ref[...], c_ref[...], (((0,), (0,)), ((), ())), preferred_element_type=jnp.float32
    )
    flat = acc.reshape(5376 * 8, 128)
    for s in range(8):
        flat[pl.ds(i * (STEP * 8) + s, STEP, stride=8), :] = prod[:, s * 128 : (s + 1) * 128]

    parts = acc.reshape(16, 8, 2, 3, ROWS * 8, 128)
    done = lax.div((i + 1) * STEP, 336)
    before = lax.div(i * STEP, 336)

    def copy_out(src, unit, count, mine):
        def put(dst, base):
            pltpu.make_async_copy(src, dst.at[pl.ds(unit - base, count)], sem).start()

        pl.when(mine)(lambda: put(keep, 0))
        pl.when(jnp.logical_not(mine) & (unit < CUT1))(lambda: put(send1, 0))
        pl.when(jnp.logical_not(mine) & (unit >= CUT1) & (unit < CUT2))(lambda: put(send2, CUT1))
        pl.when(jnp.logical_not(mine) & (unit >= CUT2))(lambda: put(send3, CUT2))

    @pl.when(done > before)
    def _():
        b = done - 1
        c2 = lax.rem(b, 2)
        y2 = lax.rem(lax.div(b, 2), 4)
        xl = lax.div(b, 8)
        sign = 1 - 2 * c2
        mine = c2 == core
        rely = lax.rem(sign * (y2 - y) + 4, 4)
        for xh in range(2):
            relx = lax.rem(sign * (2 * xh + xl - x) + 4, 4)
            copy_out(parts.at[b, :, xh, 0], pick(OFF_X, relx) + rely * 8, 8, mine)
            copy_out(parts.at[b, :, xh, 1], pick(OFF_Y, rely) + (xl * 2 + xh) * 8, 8, mine)
        for z2 in range(8):
            relz = lax.rem(sign * (z2 - z) + 8, 8)
            copy_out(parts.at[b, z2, :, 2], pick(OFF_Z, relz) + rely * 4 + xl * 2, 2, mine)

    @pl.when(i == pl.num_programs(0) - 1)
    def _():
        for out in (keep, send1, send2, send3):
            pltpu.make_async_copy(out, out, sem).wait()


def local_grad(where, hidden_in, key_cotangent):
    tokens, width = hidden_in.shape
    keys = key_cotangent.shape[1]
    shape = lambda n: jax.ShapeDtypeStruct((n, ROWS * 8, 128), jnp.float32)
    anywhere = pl.BlockSpec(memory_space=pl.ANY)
    return pl.pallas_call(
        grad_kernel,
        out_shape=(shape(UNITS), shape(CUT1), shape(CUT2 - CUT1), shape(UNITS - CUT2)),
        grid_spec=pltpu.PrefetchScalarGridSpec(
            num_scalar_prefetch=1,
            grid=(width // STEP,),
            in_specs=[
                pl.BlockSpec((tokens, STEP), lambda i, w: (0, i)),
                pl.BlockSpec((tokens, keys), lambda i, w: (0, 0)),
            ],
            out_specs=(anywhere,) * 4,
            scratch_shapes=[
                pltpu.VMEM((768, ROWS * 8, 128), jnp.float32),
                pltpu.SemaphoreType.DMA,
            ],
        ),
        compiler_params=pltpu.CompilerParams(vmem_limit_bytes=48 * 1024 * 1024),
        cost_estimate=pl.CostEstimate(
            flops=2 * tokens * width * keys,
            bytes_accessed=2 * tokens * (width + keys) + 4 * width * keys,
            transcendentals=0,
        ),
        name="local_grad",
    )(where, hidden_in, key_cotangent)


def moves(axis, hop, both=True):
    pairs = []
    for x in range(4):
        for y in range(4):
            for z in range(8):
                for c in range(2):
                    at = [x, y, z]
                    d = hop if c == 0 or not both else -hop
                    at[axis] = (at[axis] + d) % (4, 4, 8)[axis]
                    pairs.append((place(x, y, z, c), place(*at, c)))
    return pairs


def place(x, y, z, c):
    return (x // 2) * 128 + (((x % 2) * 4 + y) * 2 + c) * 8 + z


SWAP = [(place(x, y, z, c), place(x, y, z, 1 - c)) for x in range(4) for y in range(4) for z in range(8) for c in range(2)]


def go(a, axis, hop):
    return lax.ppermute(a, AXES, moves(axis, hop))


def body(hidden_in, key_cotangent):
    count_all = (
        hidden_in.shape[0] * lax.axis_size("dcn") * lax.axis_size("gx") * lax.axis_size("gy")
    )
    factor = jnp.float32(1.0 / count_all**0.5)
    x, y, z, core = coords()
    sign = 1 - 2 * core
    where = jnp.stack([x, y, z, core]).astype(jnp.int32)
    keep, send1, send2, send3 = local_grad(where, hidden_in, key_cotangent)
    got1 = lax.ppermute(send1, AXES, SWAP)
    got2 = lax.ppermute(send2, AXES, SWAP)
    got3 = lax.ppermute(send3, AXES, SWAP)

    def own(unit, count):
        mine = keep[unit : unit + count]
        if unit < CUT1:
            return mine + got1[unit : unit + count]
        if unit < CUT2:
            return mine + got2[unit - CUT1 : unit - CUT1 + count]
        return mine + got3[unit - CUT2 : unit - CUT2 + count]

    def ring4(off, axis):
        a = go(own(off[2], 32), axis, 1)
        b = go(own(off[3], 32), axis, -1)
        a = go(a + own(off[1], 32), axis, 1)
        return a + b + own(off[0], 32)

    def ring8(off, axis):
        a = go(own(off[4], 16), axis, 1)
        b = go(own(off[5], 16), axis, -1)
        a = go(a + own(off[3], 16), axis, 1)
        b = go(b + own(off[6], 16), axis, -1)
        a = go(a + own(off[2], 16), axis, 1)
        b = go(b + own(off[7], 16), axis, -1)
        a = go(a + own(off[1], 16), axis, 1)
        return a + b + own(off[0], 16)

    part_z = ring8(OFF_Z, 2)
    part_x = ring4(OFF_X, 0)
    part_y = ring4(OFF_Y, 1)

    def direct_y(part, n):
        one = go(part[n : 2 * n], 1, 1)
        back = go(part[3 * n :], 1, -1)
        far = go(part[2 * n : 3 * n], 1, 2)
        return part[:n] + one + back + far

    def along_z(part):
        def at(k):
            return lax.dynamic_index_in_dim(part, lax.rem(z + sign * k + 16, 8), axis=-3, keepdims=True)

        up = go(jnp.concatenate([at(4), at(3)], -3), 2, 2)
        down = go(jnp.concatenate([at(-3), at(-2)], -3), 2, -2)
        a2 = go(up[..., :1, :, :] + at(2), 2, 2)
        a1 = go(up[..., 1:, :, :] + at(1), 2, 1)
        b1 = go(down[..., :1, :, :] + at(-1), 2, -1)
        return (at(0) + down[..., 1:, :, :] + a2 + a1 + b1)[..., 0, :, :]

    part_x = along_z(direct_y(part_x, 8))
    part_z = direct_y(part_z, 4)
    part_y = along_z(part_y.reshape(4, 8, ROWS * 8, 128))

    both = jnp.stack([part_y.reshape(2, 2, ROWS * 8, 128), part_z.reshape(2, 2, ROWS * 8, 128)], axis=2)
    xl = lax.rem(x, 2)
    mine = lax.dynamic_index_in_dim(both, xl, keepdims=False)
    other = lax.dynamic_index_in_dim(both, 1 - xl, keepdims=False)
    both = mine + go(mine, 0, 2) + go(other, 0, 1) + go(other, 0, -1)
    partner = go(part_x, 0, 2)
    first = x < 2
    part_x = jnp.stack([jnp.where(first, part_x, partner), jnp.where(first, partner, part_x)])
    result = jnp.concatenate([part_x[:, None], both], axis=1)
    return result.reshape(2 * 3 * ROWS, 1024) * factor


def solution(mesh):
    placed = (P(AXES, None), P(AXES, None))
    return jax.shard_map(
        body, mesh=mesh, in_specs=placed, out_specs=P(("gx", "gy"), None), check_vma=False
    )
```

```python
import jax
import jax.numpy as jnp
from jax import lax
from jax.experimental import pallas as pl
from jax.experimental.pallas import tpu as pltpu
from jax.sharding import PartitionSpec as P

AXES = ("dcn", "gx", "gy")
STEP = 768
RX, RY = 8, 8
RZ = 21 - RX - RY
CX, CY, CZ = 32 * RX, 32 * RY, 16 * RZ
ORDER = (("x", 2), ("y", 2), ("z", 4), None, ("z", 5), ("z", 3), ("x", 3), ("y", 3), ("x", 1), ("y", 1),
         ("z", 6), ("z", 2), ("z", 7), ("z", 1), ("x", 0), ("y", 0), ("z", 0))
SIZE = {"x": CX, "y": CY, "z": CZ}


def layout():
    at, row, cut = {}, 0, 0
    for item in ORDER:
        if item is None:
            cut = row
        else:
            at[item] = row
            row += SIZE[item[0]]
    return at, cut, row


AT, CUT, ROWS = layout()


def pick(axis, k, n):
    value = jnp.int32(AT[axis, 0])
    for i in range(1, n):
        value = jnp.where(k == i, jnp.int32(AT[axis, i]), value)
    return value


def grad_kernel(where_ref, h_ref, c_ref, keep, send1, send2, h_buf, c_buf, acc, h_sem, c_sem, sem):
    x, y, z, core = where_ref[0], where_ref[1], where_ref[2], where_ref[3]
    steps = h_ref.shape[1] // STEP
    fetch_c = pltpu.make_async_copy(c_ref, c_buf, c_sem)
    fetch_h = [
        pltpu.make_async_copy(h_ref.at[:, pl.ds(i * STEP, STEP)], h_buf.at[i], h_sem.at[i])
        for i in range(steps)
    ]
    fetch_h[0].start()
    fetch_c.start()
    for i in range(1, steps):
        fetch_h[i].start()
    fetch_c.wait()
    flat = acc.reshape(5376 * 8, 128)
    parts = acc.reshape(16, 8, 2, 21, 8, 128)

    def copy_out(src, row, mine):
        count = 1
        for n in src.shape[:-2]:
            count *= n

        def put(dst, base):
            to = dst.at[pl.ds(row - base, count)].reshape(src.shape)
            pltpu.make_async_copy(src, to, sem).start()

        pl.when(mine)(lambda: put(keep, 0))
        pl.when(jnp.logical_not(mine) & (row < CUT))(lambda: put(send1, 0))
        pl.when(jnp.logical_not(mine) & (row >= CUT))(lambda: put(send2, CUT))

    def block_out(b):
        c2, y2, xl = b % 2, b // 2 % 4, b // 8
        sign = 1 - 2 * c2
        mine = core == c2
        rely = lax.rem(sign * (y2 - y) + 4, 4)
        for xh in range(2):
            relx = lax.rem(sign * (2 * xh + xl - x) + 4, 4)
            to_x = pick("x", relx, 4) + rely * (8 * RX)
            to_y = pick("y", rely, 4) + relx * (8 * RY)
            copy_out(parts.at[b, :, xh, pl.ds(0, RX)], to_x, mine)
            copy_out(parts.at[b, :, xh, pl.ds(RX, RY)], to_y, mine)
        for z2 in range(8):
            relz = lax.rem(sign * (z2 - z) + 8, 8)
            copy_out(
                parts.at[b, z2, :, pl.ds(RX + RY, RZ)],
                pick("z", relz, 8) + (rely * 4 + xl * 2) * RZ,
                mine,
            )

    out = 0
    for i in range(steps):
        fetch_h[i].wait()
        for j in range(0, STEP, 256):
            prod = lax.dot_general(
                h_buf[i, :, j : j + 256],
                c_buf[...],
                (((0,), (0,)), ((), ())),
                preferred_element_type=jnp.float32,
            )
            for s in range(8):
                flat[pl.ds((i * STEP + j) * 8 + s, 256, stride=8), :] = prod[:, s * 128 : (s + 1) * 128]
        while (out + 1) * 336 <= (i + 1) * STEP:
            block_out(out)
            out += 1
    for ref in (keep, send1, send2):
        pltpu.make_async_copy(ref, ref, sem).wait()


def local_grad(where, hidden_in, key_cotangent):
    tokens, width = hidden_in.shape
    keys = key_cotangent.shape[1]
    shape = lambda n: jax.ShapeDtypeStruct((n, 8, 128), jnp.float32)
    anywhere = pl.BlockSpec(memory_space=pl.ANY)
    return pl.pallas_call(
        grad_kernel,
        out_shape=(shape(ROWS), shape(CUT), shape(ROWS - CUT)),
        in_specs=[pl.BlockSpec(memory_space=pltpu.SMEM), anywhere, anywhere],
        out_specs=(anywhere,) * 3,
        scratch_shapes=[
            pltpu.VMEM((width // STEP, tokens, STEP), jnp.bfloat16),
            pltpu.VMEM((tokens, keys), jnp.bfloat16),
            pltpu.VMEM((width, 8, 128), jnp.float32),
            pltpu.SemaphoreType.DMA((width // STEP,)),
            pltpu.SemaphoreType.DMA,
            pltpu.SemaphoreType.DMA,
        ],
        compiler_params=pltpu.CompilerParams(vmem_limit_bytes=60 * 1024 * 1024),
        cost_estimate=pl.CostEstimate(
            flops=2 * tokens * width * keys,
            bytes_accessed=2 * tokens * (width + keys) + 4 * width * keys,
            transcendentals=0,
        ),
        name="local_grad",
    )(where, hidden_in, key_cotangent)


def place(x, y, z, c):
    return (x // 2) * 128 + (((x % 2) * 4 + y) * 2 + c) * 8 + z


EVERY = [(x, y, z, c) for x in range(4) for y in range(4) for z in range(8) for c in range(2)]
SWAP = [(place(x, y, z, c), place(x, y, z, 1 - c)) for x, y, z, c in EVERY]
PAIR_X = [(place(x, y, z, c), place(x ^ 1, y, z, c)) for x, y, z, c in EVERY]


def moves(axis, hop):
    pairs = []
    for x, y, z, c in EVERY:
        at = [x, y, z]
        at[axis] = (at[axis] + (hop if c == 0 else -hop)) % (4, 4, 8)[axis]
        pairs.append((place(x, y, z, c), place(*at, c)))
    return pairs


def send(a, pairs):
    return lax.ppermute(a, AXES, pairs)


def go(a, axis, hop):
    return send(a, moves(axis, hop))


def after(value, token):
    anywhere = pl.BlockSpec(memory_space=pl.ANY)
    return pl.pallas_call(
        lambda *refs: None,
        out_shape=jax.ShapeDtypeStruct(value.shape, value.dtype),
        in_specs=[anywhere, pl.BlockSpec(memory_space=pltpu.SMEM)],
        out_specs=anywhere,
        input_output_aliases={0: 0},
        cost_estimate=pl.CostEstimate(flops=0, bytes_accessed=0, transcendentals=0),
        name="after",
    )(value, token.reshape(1))


def zero(a):
    return jnp.sum(a[:1]) * jnp.float32(0)


def body(hidden_in, key_cotangent):
    count_all = (
        hidden_in.shape[0] * lax.axis_size("dcn") * lax.axis_size("gx") * lax.axis_size("gy")
    )
    factor = jnp.float32(1.0 / count_all**0.5)
    dcn, gx, z = (lax.axis_index(a) for a in AXES)
    core, y, xl = lax.rem(gx, 2), lax.rem(lax.div(gx, 2), 4), lax.div(gx, 8)
    x = dcn * 2 + xl
    sign = 1 - 2 * core
    where = jnp.stack([x, y, z, core]).astype(jnp.int32)
    keep, send1, send2 = local_grad(where, hidden_in, key_cotangent)

    got1 = send(send1, SWAP)
    got2 = send(after(send2, zero(got1)), SWAP)

    def own(name, k):
        row, count = AT[name, k], SIZE[name]
        got, base = (got1, 0) if row < CUT else (got2, CUT)
        return keep[row : row + count] + got[row - base : row - base + count]

    def ring4(name, axis):
        a = go(own(name, 2), axis, 1)
        b = go(own(name, 3), axis, -1)
        a = go(a + own(name, 1), axis, 1)
        return a + b + own(name, 0)

    def ring8(name, axis):
        a = go(own(name, 4), axis, 1)
        b = go(own(name, 5), axis, -1)
        a = go(a + own(name, 3), axis, 1)
        b = go(b + own(name, 6), axis, -1)
        a = go(a + own(name, 2), axis, 1)
        b = go(b + own(name, 7), axis, -1)
        a = go(a + own(name, 1), axis, 1)
        return a + b + own(name, 0)

    part_z = ring8("z", 2)
    part_x = ring4("x", 0)
    part_y = ring4("y", 1)

    def direct(part, axis):
        n = part.shape[0] // 4
        a = go(part[2 * n : 3 * n], axis, 1)
        b = go(part[3 * n :], axis, -1)
        a = go(a + part[n : 2 * n], axis, 1)
        return a + b + part[:n]

    part_xz = jnp.concatenate(
        [part_x.reshape(4, 8 * RX, 8, 128), part_z.reshape(4, 4 * RZ, 8, 128)], axis=1
    )
    part_xz = direct(part_xz.reshape(-1, 8, 128), 1)
    part_x, part_z = part_xz[: 8 * RX], part_xz[8 * RX :].reshape(2, 2 * RZ, 8, 128)
    part_y = direct(part_y, 0)

    both = jnp.concatenate(
        [part_x.reshape(8, RX, 8, 128), part_y.reshape(8, RY, 8, 128)], axis=1
    )

    def at(k):
        return lax.dynamic_index_in_dim(both, lax.rem(z + sign * k + 16, 8), keepdims=False)

    up = go(jnp.concatenate([at(4), at(3)]), 2, 2)
    down = go(jnp.concatenate([at(-3), at(-2)]), 2, -2)
    n = RX + RY
    a2 = go(up[:n] + at(2), 2, 2)
    a1 = go(up[n:] + at(1), 2, 1)
    b1 = go(down[:n] + at(-1), 2, -1)
    both = at(0) + down[n:] + a2 + a1 + b1
    part_z = lax.dynamic_index_in_dim(part_z, xl, keepdims=False) + send(
        lax.dynamic_index_in_dim(part_z, 1 - xl, keepdims=False), PAIR_X
    )

    mine = jnp.concatenate([both, part_z])
    theirs = go(mine, 0, 2)
    part_z = (part_z + theirs[n:]).reshape(2, RZ, 8, 128)
    first, second = jnp.where(dcn == 0, both, theirs[:n]), jnp.where(dcn == 0, theirs[:n], both)
    result = jnp.concatenate([first, part_z[0], second, part_z[1]])
    return result.reshape(-1, 1024) * factor


def solution(mesh):
    placed = (P(AXES, None), P(AXES, None))
    return jax.shard_map(
        body, mesh=mesh, in_specs=placed, out_specs=P(("gx", "gy"), None), check_vma=False
    )
```

```python
import jax
import jax.numpy as jnp
from jax import lax
from jax.experimental import pallas as pl
from jax.experimental.pallas import tpu as pltpu
from jax.sharding import PartitionSpec as P

AXES = ("dcn", "gx", "gy")
STEP = 768
RX, RY = 8, 8
RZ = 21 - RX - RY
CX, CY, CZ = 32 * RX, 32 * RY, 16 * RZ
ORDER = (("x", 2), ("y", 2), ("z", 4), None, ("z", 5), ("z", 3), ("x", 3), ("y", 3), ("x", 1), ("y", 1),
         ("z", 6), ("z", 2), ("z", 7), ("z", 1), ("x", 0), ("y", 0), ("z", 0))
SIZE = {"x": CX, "y": CY, "z": CZ}


def layout():
    at, row, cut = {}, 0, 0
    for item in ORDER:
        if item is None:
            cut = row
        else:
            at[item] = row
            row += SIZE[item[0]]
    return at, cut, row


AT, CUT, ROWS = layout()


def pick(axis, k, n):
    value = jnp.int32(AT[axis, 0])
    for i in range(1, n):
        value = jnp.where(k == i, jnp.int32(AT[axis, i]), value)
    return value


def grad_kernel(where_ref, h_ref, c_ref, keep, send1, send2, h_buf, c_buf, acc, h_sem, c_sem, sem):
    x, y, z, core = where_ref[0], where_ref[1], where_ref[2], where_ref[3]
    steps = h_ref.shape[1] // STEP
    fetch_c = pltpu.make_async_copy(c_ref, c_buf, c_sem)
    fetch_h = [
        pltpu.make_async_copy(h_ref.at[:, pl.ds(i * STEP, STEP)], h_buf.at[i], h_sem.at[i])
        for i in range(steps)
    ]
    fetch_h[0].start()
    fetch_c.start()
    fetch_c.wait()
    flat = acc.reshape(5376 * 8, 128)
    parts = acc.reshape(16, 8, 2, 21, 8, 128)

    def put(src, row, dst, base):
        count = 1
        for n in src.shape[:-2]:
            count *= n
        to = dst.at[pl.ds(row - base, count)].reshape(src.shape)
        pltpu.make_async_copy(src, to, sem).start()

    def block_out(b):
        c2, y2, xl = b % 2, b // 2 % 4, b // 8
        sign = 1 - 2 * c2
        rely = lax.rem(sign * (y2 - y) + 4, 4)
        copies = []
        for xh in range(2):
            relx = lax.rem(sign * (2 * xh + xl - x) + 4, 4)
            to_x = pick("x", relx, 4) + rely * (8 * RX)
            to_y = pick("y", rely, 4) + relx * (8 * RY)
            copies.append((parts.at[b, :, xh, pl.ds(0, RX)], to_x))
            copies.append((parts.at[b, :, xh, pl.ds(RX, RY)], to_y))
        for z2 in range(8):
            relz = lax.rem(sign * (z2 - z) + 8, 8)
            to_z = pick("z", relz, 8) + (rely * 4 + xl * 2) * RZ
            copies.append((parts.at[b, z2, :, pl.ds(RX + RY, RZ)], to_z))

        @pl.when(core == c2)
        def _():
            for src, row in copies:
                put(src, row, keep, 0)

        @pl.when(core != c2)
        def _():
            for src, row in copies:
                pl.when(row < CUT)(lambda: put(src, row, send1, 0))
                pl.when(row >= CUT)(lambda: put(src, row, send2, CUT))

    out = 0
    for i in range(steps):
        fetch_h[i].wait()
        for ahead in (1, 2) if i == 0 else (i + 2,):
            if ahead < steps:
                fetch_h[ahead].start()
        for j in range(0, STEP, 256):
            prod = lax.dot_general(
                h_buf[i, :, j : j + 256],
                c_buf[...],
                (((0,), (0,)), ((), ())),
                preferred_element_type=jnp.float32,
            )
            for s in range(8):
                flat[pl.ds((i * STEP + j) * 8 + s, 256, stride=8), :] = prod[:, s * 128 : (s + 1) * 128]
        while (out + 1) * 336 <= (i + 1) * STEP:
            block_out(out)
            out += 1
    for ref in (keep, send1, send2):
        pltpu.make_async_copy(ref, ref, sem).wait()


def local_grad(where, hidden_in, key_cotangent):
    tokens, width = hidden_in.shape
    keys = key_cotangent.shape[1]
    shape = lambda n: jax.ShapeDtypeStruct((n, 8, 128), jnp.float32)
    anywhere = pl.BlockSpec(memory_space=pl.ANY)
    return pl.pallas_call(
        grad_kernel,
        out_shape=(shape(ROWS), shape(CUT), shape(ROWS - CUT)),
        in_specs=[pl.BlockSpec(memory_space=pltpu.SMEM), anywhere, anywhere],
        out_specs=(anywhere,) * 3,
        scratch_shapes=[
            pltpu.VMEM((width // STEP, tokens, STEP), jnp.bfloat16),
            pltpu.VMEM((tokens, keys), jnp.bfloat16),
            pltpu.VMEM((width, 8, 128), jnp.float32),
            pltpu.SemaphoreType.DMA((width // STEP,)),
            pltpu.SemaphoreType.DMA,
            pltpu.SemaphoreType.DMA,
        ],
        compiler_params=pltpu.CompilerParams(vmem_limit_bytes=60 * 1024 * 1024),
        cost_estimate=pl.CostEstimate(
            flops=2 * tokens * width * keys,
            bytes_accessed=2 * tokens * (width + keys) + 4 * width * keys,
            transcendentals=0,
        ),
        name="local_grad",
    )(where, hidden_in, key_cotangent)


def place(x, y, z, c):
    return (x // 2) * 128 + (((x % 2) * 4 + y) * 2 + c) * 8 + z


EVERY = [(x, y, z, c) for x in range(4) for y in range(4) for z in range(8) for c in range(2)]
SWAP = [(place(x, y, z, c), place(x, y, z, 1 - c)) for x, y, z, c in EVERY]
PAIR_X = [(place(x, y, z, c), place(x ^ 1, y, z, c)) for x, y, z, c in EVERY]


def moves(axis, hop):
    pairs = []
    for x, y, z, c in EVERY:
        at = [x, y, z]
        at[axis] = (at[axis] + (hop if c == 0 else -hop)) % (4, 4, 8)[axis]
        pairs.append((place(x, y, z, c), place(*at, c)))
    return pairs


def send(a, pairs):
    return lax.ppermute(a, AXES, pairs)


def go(a, axis, hop):
    return send(a, moves(axis, hop))


def after(value, token):
    anywhere = pl.BlockSpec(memory_space=pl.ANY)
    return pl.pallas_call(
        lambda *refs: None,
        out_shape=jax.ShapeDtypeStruct(value.shape, value.dtype),
        in_specs=[anywhere, pl.BlockSpec(memory_space=pltpu.SMEM)],
        out_specs=anywhere,
        input_output_aliases={0: 0},
        cost_estimate=pl.CostEstimate(flops=0, bytes_accessed=0, transcendentals=0),
        name="after",
    )(value, token.reshape(1))


def zero(a):
    return jnp.sum(a[:1]) * jnp.float32(0)


def body(hidden_in, key_cotangent):
    count_all = (
        hidden_in.shape[0] * lax.axis_size("dcn") * lax.axis_size("gx") * lax.axis_size("gy")
    )
    factor = jnp.float32(1.0 / count_all**0.5)
    dcn, gx, z = (lax.axis_index(a) for a in AXES)
    core, y, xl = lax.rem(gx, 2), lax.rem(lax.div(gx, 2), 4), lax.div(gx, 8)
    x = dcn * 2 + xl
    sign = 1 - 2 * core
    where = jnp.stack([x, y, z, core]).astype(jnp.int32)
    keep, send1, send2 = local_grad(where, hidden_in, key_cotangent)

    got1 = send(send1, SWAP)
    got2 = send(after(send2, zero(got1)), SWAP)

    def own(name, k):
        row, count = AT[name, k], SIZE[name]
        got, base = (got1, 0) if row < CUT else (got2, CUT)
        return keep[row : row + count] + got[row - base : row - base + count]

    def ring4(name, axis):
        a = go(own(name, 2), axis, 1)
        b = go(own(name, 3), axis, -1)
        a = go(a + own(name, 1), axis, 1)
        return a + b + own(name, 0)

    def ring8(name, axis):
        a = go(own(name, 4), axis, 1)
        b = go(own(name, 5), axis, -1)
        a = go(a + own(name, 3), axis, 1)
        b = go(b + own(name, 6), axis, -1)
        a = go(a + own(name, 2), axis, 1)
        b = go(b + own(name, 7), axis, -1)
        a = go(a + own(name, 1), axis, 1)
        return a + b + own(name, 0)

    part_z = ring8("z", 2)
    part_x = ring4("x", 0)
    part_y = ring4("y", 1)

    def direct(part, axis):
        n = part.shape[0] // 4
        a = go(part[2 * n : 3 * n], axis, 1)
        b = go(part[3 * n :], axis, -1)
        a = go(a + part[n : 2 * n], axis, 1)
        return a + b + part[:n]

    part_xz = jnp.concatenate(
        [part_x.reshape(4, 8 * RX, 8, 128), part_z.reshape(4, 4 * RZ, 8, 128)], axis=1
    )
    part_xz = direct(part_xz.reshape(-1, 8, 128), 1)
    part_x, part_z = part_xz[: 8 * RX], part_xz[8 * RX :].reshape(2, 2 * RZ, 8, 128)
    part_y = direct(part_y, 0)

    both = jnp.concatenate(
        [part_x.reshape(8, RX, 8, 128), part_y.reshape(8, RY, 8, 128)], axis=1
    )

    def at(k):
        return lax.dynamic_index_in_dim(both, lax.rem(z + sign * k + 16, 8), keepdims=False)

    up = go(jnp.concatenate([at(4), at(3)]), 2, 2)
    down = go(jnp.concatenate([at(-3), at(-2)]), 2, -2)
    n = RX + RY
    a2 = go(up[:n] + at(2), 2, 2)
    a1 = go(up[n:] + at(1), 2, 1)
    b1 = go(down[:n] + at(-1), 2, -1)
    both = at(0) + down[n:] + a2 + a1 + b1
    part_z = lax.dynamic_index_in_dim(part_z, xl, keepdims=False) + send(
        lax.dynamic_index_in_dim(part_z, 1 - xl, keepdims=False), PAIR_X
    )

    mine = jnp.concatenate([both, part_z])
    theirs = go(mine, 0, 2)
    part_z = (part_z + theirs[n:]).reshape(2, RZ, 8, 128)
    first, second = jnp.where(dcn == 0, both, theirs[:n]), jnp.where(dcn == 0, theirs[:n], both)
    result = jnp.concatenate([first, part_z[0], second, part_z[1]])
    return result.reshape(-1, 1024) * factor


def solution(mesh):
    placed = (P(AXES, None), P(AXES, None))
    return jax.shard_map(
        body, mesh=mesh, in_specs=placed, out_specs=P(("gx", "gy"), None), check_vma=False
    )
```
